512 devices in a mesh: dp: 64 (over y, z), proto: 8 (over x, core).
Axes of the slice: x: 4, y: 8, z: 8, core: 2. Of those that a mesh axis runs over, the one named last changes fastest.
Arguments:
- features: bfloat16 [32768, 256], P('dp'), may hold values from -120 to 120
- prototypes: bfloat16 [256, 131072], P(None, ('proto', 'dp')), may hold values from -40 to 40
Outputs:
- row_log: float32 [32768], P('dp')
- col_log: float32 [131072], P(('proto', 'dp'))
The draws below stay inside these ranges and needn't reach their ends.
All inputs are finite; a program needn't handle non-finite values.
Results may differ from the reference program's by a relative error of at most 0.00033.
Values may be sent and summed in bfloat16 or wider, within the bound.
A program may use at most 128 MiB of HBM per device.

```python
import math
import jax
import jax.numpy as jnp
from jax import lax

D = 256
K = 131072
ITERS = 3
IMAGES = 32768
N_DP = 64
N_PROTO = 8


def group_layout(key):
    group_count = max(4, min(64, IMAGES // 64))
    key_centers, key_assign = jax.random.split(key)
    centers = jnp.clip(jax.random.normal(key_centers, (group_count, D), jnp.float32), -4.0, 4.0)
    assign = jax.random.randint(key_assign, (K,), 0, group_count)
    return (centers, assign, group_count)


def draw_prototypes(key, part):
    centers, assign, group_count = group_layout(key)
    key = jax.random.fold_in(key, 11)
    key_noise, key_pull, key_factor = jax.random.split(key, 3)
    center_cols = jnp.take(centers, assign, axis=0).T
    noise = jnp.clip(jax.random.normal(key_noise, (D, K), jnp.float32), -4.0, 4.0)
    pull = jax.random.uniform(key_pull, (K,), jnp.float32, 0.8, 2.5)
    factor = jnp.exp(jax.random.uniform(key_factor, (K,), jnp.float32, 0.0, math.log(10.0)))
    mixed = (pull[None, :] * center_cols + noise) / (1.0 + pull[None, :])
    return (mixed * factor[None, :]).astype(jnp.bfloat16)


def draw_features(key, part):
    centers, assign, group_count = group_layout(key)
    key = jax.random.fold_in(key, 23)
    key_coin, key_wide, key_narrow, key_strength, key_noise, key_rows = jax.random.split(key, 6)
    coin = jax.random.randint(key_coin, (IMAGES,), 0, 2)
    wide = jax.random.randint(key_wide, (IMAGES,), 0, group_count)
    narrow = jax.random.randint(key_narrow, (IMAGES,), 0, max(1, group_count // 4))
    picks = jnp.where(coin == 1, wide, narrow)
    matched = jnp.take(centers, picks, axis=0)
    strength = jax.random.uniform(key_strength, (IMAGES, 1), jnp.float32, 0.7, 1.8)
    noise = jnp.clip(jax.random.normal(key_noise, (IMAGES, D), jnp.float32), -4.0, 4.0)
    image_row_scale = jnp.exp(jax.random.uniform(key_rows, (IMAGES, 1), jnp.float32, 0.0, math.log(10.0)))
    return ((strength * matched + noise) * image_row_scale).astype(jnp.bfloat16)


def setup_inputs(seed: int = 0) -> dict:
    arg_keys = jax.random.split(jax.random.key(seed), 3)
    features = draw_features(jax.random.fold_in(arg_keys[2], 71), 0)
    prototypes = draw_prototypes(jax.random.fold_in(arg_keys[2], 71), 0)
    return {"features": features, "prototypes": prototypes}


sharpening_divisor = 0.07
epsilon_guard = 1e-06

def reference(features, prototypes):
    values = features.astype(jnp.float32)
    unit = (values / jnp.sqrt(lax.optimization_barrier(jnp.sum(values * values, axis=1, keepdims=True)) + epsilon_guard)).astype(jnp.bfloat16)
    width_block = K // (N_PROTO * N_DP)
    blocks = K // width_block
    image_batch = features.shape[0]

    def make_block(index):
        piece = lax.dynamic_slice_in_dim(prototypes, (index * width_block).astype(jnp.int32), width_block, 1)
        cluster_tally = piece.astype(jnp.float32)
        equalizing_multiplier = 1.0 / jnp.sqrt(lax.optimization_barrier(jnp.sum(cluster_tally * cluster_tally, axis=0)) + epsilon_guard) / sharpening_divisor
        scores = jnp.dot(unit, piece, preferred_element_type=jnp.float32) * equalizing_multiplier[None, :]
        return jnp.exp(scores).astype(jnp.bfloat16)
    tiles = lax.map(make_block, jnp.arange(blocks, dtype=jnp.int32))
    weight = jnp.ones((image_batch,), jnp.float32)
    colscale = jnp.ones((blocks, width_block), jnp.float32)
    for step in range(ITERS):

        def column_block(block, weight=weight):
            return lax.optimization_barrier(jnp.sum(block.astype(jnp.float32) * weight[:, None], axis=0))
        colscale = 1.0 / (K * lax.map(column_block, tiles))

        def row_block(total, pair):
            block, scales = pair
            return (total + lax.optimization_barrier(jnp.sum(block.astype(jnp.float32) * scales[None, :], axis=1)), None)
        sample_mass, unused = lax.scan(row_block, jnp.zeros((image_batch,), jnp.float32), (tiles, colscale))
        weight = 1.0 / (image_batch * sample_mass)
    row_log = jnp.log(image_batch * weight)
    col_log = jnp.log(float(K) * float(image_batch) * colscale.reshape(K))
    return (row_log, col_log)
```

```python
import jax
import jax.numpy as jnp
from jax import lax
from jax.experimental import pallas as pl
from jax.experimental.pallas import tpu as pltpu
from jax.sharding import PartitionSpec as P

K = 131072
IMAGES = 32768
ITERS = 3
NY = 8
NZ = 8
NP = 8
ROWS = 512
COLS = 256
HALF = ROWS // 2
LANES = 128
EPS = 1e-6
LOG2E = 1.4426950408889634
SHARP = 0.07
F32 = jnp.float32
BF16 = jnp.bfloat16
MESH = pl.DeviceIdType.MESH


def near_first(k):
    return lax.rem(jnp.where(lax.rem(k, 2) == 1, (k + 1) // 2, 8 - k // 2), 8)


def kernel(
    feat, proto, row_out, col_out,
    tile, unit, piece, scale, colacc, colbuf, colval, rowpart, rowsum, rowbuf, rowall, lastz, lastp, weight,
    unit_send, unit_recv, core_send, core_recv, piece_send, piece_recv,
    col_send, col_recv, rowp_send, rowp_recv, rowz_send, rowz_recv,
):
    dp = lax.axis_index("dp")
    me_p = lax.axis_index("proto")
    y, z = dp // NZ, lax.rem(dp, NZ)
    core = lax.rem(me_p, 2)

    def y_peer(d):
        return (lax.rem(y + d, NY) * NZ + z, me_p)

    def z_peer(d):
        return (y * NZ + lax.rem(z + d, NZ), me_p)

    def p_peer(d):
        return (dp, lax.rem(me_p + d, NP))

    other_core = (dp, me_p + 1 - 2 * core)

    barrier = pltpu.get_barrier_semaphore()

    def greet(d, _):
        pl.semaphore_signal(barrier, inc=1, device_id=y_peer(d), device_id_type=MESH)
        pl.semaphore_signal(barrier, inc=1, device_id=z_peer(d), device_id_type=MESH)
        pl.semaphore_signal(barrier, inc=1, device_id=p_peer(d), device_id_type=MESH)
        return 0

    lax.fori_loop(1, 8, greet, 0)

    values = feat[...].astype(F32)
    norm = jnp.sqrt(jnp.sum(values * values, axis=1, keepdims=True) + EPS)
    unit[pl.ds(z, 1)] = (values / norm).astype(BF16)[None]
    piece[pl.ds(y, 1)] = proto[...][None]
    colacc[...] = jnp.zeros_like(colacc)

    pl.semaphore_wait(barrier, 21)

    half = pl.ds(pl.multiple_of(core * HALF, HALF), HALF)

    def piece_copy(d):
        return pltpu.make_async_remote_copy(
            src_ref=piece.at[y], dst_ref=piece.at[y], send_sem=piece_send.at[d], recv_sem=piece_recv.at[d],
            device_id=y_peer(d), device_id_type=MESH)

    def unit_copy(d):
        return pltpu.make_async_remote_copy(
            src_ref=unit.at[z, half], dst_ref=unit.at[z, half], send_sem=unit_send.at[d], recv_sem=unit_recv.at[d],
            device_id=z_peer(d), device_id_type=MESH)

    def core_copy(d):
        source = lax.rem(z - d + NZ, NZ)
        return pltpu.make_async_remote_copy(
            src_ref=unit.at[source, half], dst_ref=unit.at[source, half],
            send_sem=core_send.at[d], recv_sem=core_recv.at[d],
            device_id=other_core, device_id_type=MESH)

    def start(k, _):
        d = near_first(k)
        unit_copy(d).start()
        piece_copy(d).start()
        return 0

    lax.fori_loop(1, 8, start, 0)

    def block(us, vs):
        scores = jnp.dot(unit[us], piece[vs], preferred_element_type=F32) * scale[vs]
        e = jnp.exp2(scores)
        tile[vs, pl.ds(pl.multiple_of(us * ROWS, ROWS), ROWS), :] = e
        colacc[vs] += jnp.sum(e.reshape(ROWS // 8, 8, COLS), axis=0)

    def arrive(k, _):
        d = near_first(k)

        @pl.when(k > 0)
        def _():
            unit_copy(d).wait_recv()
            core_copy(d).start()
            piece_copy(d).wait_recv()

        vs = lax.rem(y - d + NY, NY)
        v = piece[vs].astype(F32)
        scale[vs] = (LOG2E / SHARP) / jnp.sqrt(jnp.sum(v * v, axis=0, keepdims=True) + EPS)

        @pl.when(k > 0)
        def _():
            core_copy(d).wait_recv()

        def pair(t, _):
            ku = jnp.where(t <= k, k, t - k - 1)
            kv = jnp.where(t <= k, t, k)
            block(lax.rem(z - near_first(ku) + NZ, NZ), lax.rem(y - near_first(kv) + NY, NY))
            return 0

        lax.fori_loop(0, 2 * k + 1, pair, 0)
        return 0

    lax.fori_loop(0, 8, arrive, 0)

    def col_copy(step, d):
        return pltpu.make_async_remote_copy(
            src_ref=colbuf.at[step, y], dst_ref=colbuf.at[step, y],
            send_sem=col_send.at[step, d], recv_sem=col_recv.at[step, d],
            device_id=y_peer(d), device_id_type=MESH)

    def rowp_copy(step, d):
        return pltpu.make_async_remote_copy(
            src_ref=rowbuf.at[step, me_p], dst_ref=rowbuf.at[step, me_p],
            send_sem=rowp_send.at[step, d], recv_sem=rowp_recv.at[step, d],
            device_id=p_peer(d), device_id_type=MESH)

    def rowz_copy(step, d):
        return pltpu.make_async_remote_copy(
            src_ref=rowall.at[step, z], dst_ref=rowall.at[step, z],
            send_sem=rowz_send.at[step, d], recv_sem=rowz_recv.at[step, d],
            device_id=z_peer(d), device_id_type=MESH)

    def lastz_copy(d):
        return pltpu.make_async_remote_copy(
            src_ref=rowpart.at[lax.rem(z + d, NZ)], dst_ref=lastz.at[z],
            send_sem=rowz_send.at[ITERS - 1, d], recv_sem=rowz_recv.at[ITERS - 1, d],
            device_id=z_peer(d), device_id_type=MESH)

    def lastp_copy(d):
        return pltpu.make_async_remote_copy(
            src_ref=lastp.at[me_p], dst_ref=lastp.at[me_p],
            send_sem=rowp_send.at[ITERS - 1, d], recv_sem=rowp_recv.at[ITERS - 1, d],
            device_id=p_peer(d), device_id_type=MESH)

    def exchange(copy):
        for d in range(1, 8):
            copy(d).start()
        for d in range(1, 8):
            copy(d).wait_recv()

    def column_pass():
        def body(i, acc):
            rows = pl.ds(pl.multiple_of(i * LANES, LANES), LANES)
            w = jnp.broadcast_to(weight[pl.ds(i, 1), :], (LANES, LANES)).T
            out = []
            for j in range(2 * NY):
                t = tile[j // 2, rows, (j % 2) * LANES:(j % 2 + 1) * LANES] * w
                out.append(acc[j] + jnp.sum(t.reshape(LANES // 8, 8, LANES), axis=0))
            return tuple(out)

        acc = lax.fori_loop(0, NZ * ROWS // LANES, body, tuple(jnp.zeros((8, LANES), F32) for _ in range(2 * NY)))
        for j in range(2 * NY):
            colacc[j // 2, :, (j % 2) * LANES:(j % 2 + 1) * LANES] = acc[j]

    def row_pass():
        def body(i, _):
            rows = pl.ds(pl.multiple_of(i * LANES, LANES), LANES)
            acc = None
            for j in range(2 * NY):
                lanes = slice((j % 2) * LANES, (j % 2 + 1) * LANES)
                t = tile[j // 2, rows, lanes] * colval[j // 2:j // 2 + 1, lanes]
                acc = t if acc is None else acc + t
            rowpart[i // 4, pl.ds(lax.rem(i, 4), 1), :] = jnp.sum(acc.T, axis=0, keepdims=True)
            return 0

        lax.fori_loop(0, NZ * ROWS // LANES, body, 0)

    for step in range(ITERS):
        if step > 0:
            column_pass()
        colbuf[step, pl.ds(y, 1)] = jnp.sum(colacc[...], axis=1)[None]
        exchange(lambda d: col_copy(step, d))
        colval[...] = 1.0 / (K * jnp.sum(colbuf[step], axis=0))
        row_pass()
        if step < ITERS - 1:
            rowbuf[step, pl.ds(me_p, 1)] = rowpart[...][None]
            exchange(lambda d: rowp_copy(step, d))
            rowall[step, pl.ds(z, 1)] = jnp.sum(rowbuf[step], axis=0)[None]
            exchange(lambda d: rowz_copy(step, d))
            w = 1.0 / (IMAGES * jnp.sum(rowall[step], axis=0))
            for i in range(NZ):
                weight[4 * i:4 * i + 4, :] = w[i]
        else:
            lastz[pl.ds(z, 1)] = rowpart[pl.ds(z, 1)]
            exchange(lastz_copy)
            lastp[pl.ds(me_p, 1)] = jnp.sum(lastz[...], axis=0)[None]
            exchange(lastp_copy)
            row_out[...] = jnp.log(IMAGES * (1.0 / (IMAGES * jnp.sum(lastp[...], axis=0))))
            col_out[...] = jnp.log(float(K) * float(IMAGES) * colval[pl.ds(y, 1), :])

    def drain(d, _):
        unit_copy(d).wait_send()
        piece_copy(d).wait_send()
        core_copy(d).wait_send()
        for step in range(ITERS):
            col_copy(step, d).wait_send()
            if step < ITERS - 1:
                rowp_copy(step, d).wait_send()
                rowz_copy(step, d).wait_send()
        lastz_copy(d).wait_send()
        lastp_copy(d).wait_send()
        return 0

    lax.fori_loop(1, 8, drain, 0)


def local(features, prototypes):
    vmem = pl.BlockSpec(memory_space=pltpu.VMEM)
    row_log, col_log = pl.pallas_call(
        kernel,
        out_shape=(
            jax.ShapeDtypeStruct((ROWS // LANES, LANES), F32),
            jax.ShapeDtypeStruct((1, COLS), F32),
        ),
        in_specs=[vmem, vmem],
        out_specs=(vmem, vmem),
        scratch_shapes=[
            pltpu.VMEM((NY, NZ * ROWS, COLS), F32),
            pltpu.VMEM((NZ, ROWS, 256), BF16),
            pltpu.VMEM((NY, 256, COLS), BF16),
            pltpu.VMEM((NY, 1, COLS), F32),
            pltpu.VMEM((NY, 8, COLS), F32),
            pltpu.VMEM((ITERS, NY, NY, COLS), F32),
            pltpu.VMEM((NY, COLS), F32),
            pltpu.VMEM((NZ, 4, LANES), F32),
            pltpu.VMEM((NZ, 4, LANES), F32),
            pltpu.VMEM((ITERS - 1, NP, NZ, 4, LANES), F32),
            pltpu.VMEM((ITERS - 1, NZ, NZ, 4, LANES), F32),
            pltpu.VMEM((NZ, 4, LANES), F32),
            pltpu.VMEM((NP, 4, LANES), F32),
            pltpu.VMEM((NZ * 4, LANES), F32),
        ]
        + [pltpu.SemaphoreType.DMA((8,))] * 6
        + [pltpu.SemaphoreType.DMA((ITERS, 8))] * 6,
        compiler_params=pltpu.CompilerParams(
            collective_id=0, has_side_effects=True, vmem_limit_bytes=56 * 2**20
        ),
        cost_estimate=pl.CostEstimate(
            flops=2 * 4096 * 2048 * 256, bytes_accessed=2**20, transcendentals=4096 * 2048
        ),
        name="sinkhorn",
    )(features, prototypes)
    return row_log.reshape(ROWS), col_log.reshape(COLS)


def solution(mesh):
    in_specs = (P("dp", None), P(None, ("proto", "dp")))
    out_specs = (P("dp"), P(("proto", "dp")))
    return jax.shard_map(local, mesh=mesh, in_specs=in_specs, out_specs=out_specs, check_vma=False)
```

```python
import jax
import jax.numpy as jnp
from jax import lax
from jax.experimental import pallas as pl
from jax.experimental.pallas import tpu as pltpu
from jax.sharding import PartitionSpec as P

K = 131072
IMAGES = 32768
ITERS = 3
NY = 8
NZ = 8
NP = 8
ROWS = 512
COLS = 256
HALF = ROWS // 2
CHUNKS = 2
BLOCK = 512
NBLOCK = NZ * ROWS // BLOCK
PER = BLOCK // 128
LANES = 128
EPS = 1e-6
LOG2E = 1.4426950408889634
SHARP = 0.07
F32 = jnp.float32
BF16 = jnp.bfloat16
MESH = pl.DeviceIdType.MESH


def near_first(k):
    return lax.rem(jnp.where(lax.rem(k, 2) == 1, (k + 1) // 2, 8 - k // 2), 8)


def kernel(
    feat, proto, row_out, col_out,
    tile, unit, piece, scale, colacc, colbuf, colval, rowpart, rowbuf, rowall, lastz, lastp, weight, wide,
    unit_send, unit_recv, core_send, core_recv, piece_send, piece_recv,
    col_send, col_recv, rowp_send, rowp_recv, rowz_send, rowz_recv, wcore_send, wcore_recv,
):
    dp = lax.axis_index("dp")
    me_p = lax.axis_index("proto")
    y, z = dp // NZ, lax.rem(dp, NZ)
    core = lax.rem(me_p, 2)

    def y_peer(d):
        return (lax.rem(y + d, NY) * NZ + z, me_p)

    def z_peer(d):
        return (y * NZ + lax.rem(z + d, NZ), me_p)

    def p_peer(d):
        return (dp, lax.rem(me_p + d, NP))

    other_core = (dp, me_p + 1 - 2 * core)

    barrier = pltpu.get_barrier_semaphore()

    def greet(d, _):
        pl.semaphore_signal(barrier, inc=1, device_id=y_peer(d), device_id_type=MESH)
        pl.semaphore_signal(barrier, inc=1, device_id=z_peer(d), device_id_type=MESH)
        pl.semaphore_signal(barrier, inc=1, device_id=p_peer(d), device_id_type=MESH)
        return 0

    lax.fori_loop(1, 8, greet, 0)

    values = feat[...].astype(F32)
    norm = jnp.sqrt(jnp.sum(values * values, axis=1, keepdims=True) + EPS)
    unit[pl.ds(z, 1)] = (values / norm).astype(BF16)[None]
    piece[pl.ds(y, 1)] = proto[...][None]
    colacc[...] = jnp.zeros_like(colacc)

    def set_scale(vs):
        v = piece[vs].astype(F32)
        scale[vs] = (LOG2E / SHARP) / jnp.sqrt(jnp.sum(v * v, axis=0, keepdims=True) + EPS)

    set_scale(y)
    pl.semaphore_wait(barrier, 21)

    def chunk(c):
        return pl.ds(c * (256 // CHUNKS), 256 // CHUNKS)

    def half_chunk(c):
        rows = 256 // CHUNKS
        return pl.ds(pl.multiple_of(core * HALF + c * rows, rows), rows)

    def way(r):
        return 1 if r == 0 else 7

    def piece_copy(r, s, c):
        slot = lax.rem(y + 8 * (s - 1) - way(r) * (s - 1), NY)
        return pltpu.make_async_remote_copy(
            src_ref=piece.at[slot, chunk(c)], dst_ref=piece.at[slot, chunk(c)],
            send_sem=piece_send.at[r, s, c], recv_sem=piece_recv.at[r, s, c],
            device_id=y_peer(way(r)), device_id_type=MESH)

    def unit_copy(r, s, c):
        slot = lax.rem(z + 8 * (s - 1) - way(r) * (s - 1), NZ)
        return pltpu.make_async_remote_copy(
            src_ref=unit.at[slot, half_chunk(c)], dst_ref=unit.at[slot, half_chunk(c)],
            send_sem=unit_send.at[r, s, c], recv_sem=unit_recv.at[r, s, c],
            device_id=z_peer(way(r)), device_id_type=MESH)

    def core_copy(r, s, c):
        slot = lax.rem(z + 8 * s - way(r) * s, NZ)
        return pltpu.make_async_remote_copy(
            src_ref=unit.at[slot, half_chunk(c)], dst_ref=unit.at[slot, half_chunk(c)],
            send_sem=core_send.at[r, s, c], recv_sem=core_recv.at[r, s, c],
            device_id=other_core, device_id_type=MESH)

    for c in range(CHUNKS):
        for r in range(2):
            unit_copy(r, 1, c).start()
            piece_copy(r, 1, c).start()

    def slot_pair(t):
        k = sum((t >= j * j).astype(jnp.int32) for j in range(1, 8))
        rest = t - k * k
        ku = jnp.where(rest <= k, k, rest - k - 1)
        kv = jnp.where(rest <= k, rest, k)
        return lax.rem(z - near_first(ku) + NZ, NZ), lax.rem(y - near_first(kv) + NY, NY)

    def four(b, _):
        for q in range(4):
            us, vs = slot_pair(4 * b + q)
            e = jnp.exp2(jnp.dot(unit[us], piece[vs], preferred_element_type=F32) * scale[vs])
            tile[vs, pl.ds(pl.multiple_of(us * ROWS, ROWS), ROWS), :] = e
            colacc[vs] += jnp.sum(e.reshape(ROWS // 8, 8, COLS), axis=0)
        return 0

    def arrive(s, _):
        for c in range(CHUNKS):
            for r in range(2):
                @pl.when(s + r <= 4)
                def _():
                    unit_copy(r, s, c).wait_recv()
                    core_copy(r, s, c).start()

                    @pl.when(s + r < 4)
                    def _():
                        unit_copy(r, s + 1, c).start()

                    piece_copy(r, s, c).wait_recv()

                    @pl.when(s + r < 4)
                    def _():
                        piece_copy(r, s + 1, c).start()

        set_scale(lax.rem(y + 7 * s, NY))

        @pl.when(s < 4)
        def _():
            set_scale(lax.rem(y + s, NY))

        for c in range(CHUNKS):
            for r in range(2):
                @pl.when(s + r <= 4)
                def _():
                    core_copy(r, s, c).wait_recv()

        before = 2 * s - 1
        now = jnp.minimum(2 * s + 1, 8)
        lax.fori_loop(before * before // 4, now * now // 4, four, 0)
        return 0

    lax.fori_loop(1, 5, arrive, 0)

    def col_copy(step, d):
        return pltpu.make_async_remote_copy(
            src_ref=colbuf.at[step, y], dst_ref=colbuf.at[step, y],
            send_sem=col_send.at[step, d], recv_sem=col_recv.at[step, d],
            device_id=y_peer(d), device_id_type=MESH)

    def rowp_copy(step, d):
        target = lax.rem(me_p + d, NP)
        return pltpu.make_async_remote_copy(
            src_ref=rowpart.at[pl.ds(4 * lax.rem(target, 2), 4)], dst_ref=rowbuf.at[step, me_p],
            send_sem=rowp_send.at[step, d], recv_sem=rowp_recv.at[step, d],
            device_id=p_peer(d), device_id_type=MESH)

    def rowz_copy(step, d):
        return pltpu.make_async_remote_copy(
            src_ref=rowall.at[step, z], dst_ref=rowall.at[step, z],
            send_sem=rowz_send.at[step, d], recv_sem=rowz_recv.at[step, d],
            device_id=z_peer(d), device_id_type=MESH)

    def weight_copy(step):
        return pltpu.make_async_remote_copy(
            src_ref=weight.at[step, core], dst_ref=weight.at[step, core],
            send_sem=wcore_send.at[step], recv_sem=wcore_recv.at[step],
            device_id=other_core, device_id_type=MESH)

    def lastz_copy(d):
        return pltpu.make_async_remote_copy(
            src_ref=rowpart.at[lax.rem(z + d, NZ)], dst_ref=lastz.at[z],
            send_sem=rowz_send.at[ITERS - 1, d], recv_sem=rowz_recv.at[ITERS - 1, d],
            device_id=z_peer(d), device_id_type=MESH)

    def lastp_copy(d):
        return pltpu.make_async_remote_copy(
            src_ref=lastp.at[me_p], dst_ref=lastp.at[me_p],
            send_sem=rowp_send.at[ITERS - 1, d], recv_sem=rowp_recv.at[ITERS - 1, d],
            device_id=p_peer(d), device_id_type=MESH)

    def exchange(copy):
        for d in range(1, 8):
            copy(d).start()
        for d in range(1, 8):
            copy(d).wait_recv()

    def rows_of(i, q):
        return pl.ds(pl.multiple_of(i * BLOCK + q * LANES, LANES), LANES)

    def column_pass(step):
        def spread(h, i):
            return [jnp.broadcast_to(weight[step, h, pl.ds(i * PER + q, 1), :], (LANES, LANES)).T for q in range(PER)]

        def half_pass(h, acc):
            first = h * (NBLOCK // 2)
            for q, w in enumerate(spread(h, 0)):
                wide[0, q] = w

            def body(i, acc):
                acc = list(acc)
                ws = [wide[lax.rem(i, 2), q] for q in range(PER)]
                ahead = spread(h, jnp.minimum(i + 1, NBLOCK // 2 - 1))
                for q in range(PER):
                    for j in range(2 * NY):
                        t = tile[j // 2, rows_of(first + i, q), (j % 2) * LANES:(j % 2 + 1) * LANES] * ws[q]
                        acc[j] = acc[j] + jnp.sum(t.reshape(LANES // 8, 8, LANES), axis=0)
                for q in range(PER):
                    wide[1 - lax.rem(i, 2), q] = ahead[q]
                return tuple(acc)

            return lax.fori_loop(0, NBLOCK // 2, body, acc)

        acc = half_pass(core, tuple(jnp.zeros((8, LANES), F32) for _ in range(2 * NY)))
        weight_copy(step).wait_recv()
        acc = half_pass(1 - core, acc)
        for j in range(2 * NY):
            colacc[j // 2, :, (j % 2) * LANES:(j % 2 + 1) * LANES] = acc[j]

    def row_pass():
        def work(i):
            out = []
            for q in range(PER):
                acc = None
                for j in range(2 * NY):
                    lanes = slice((j % 2) * LANES, (j % 2 + 1) * LANES)
                    t = tile[j // 2, rows_of(i, q), lanes] * colval[j // 2:j // 2 + 1, lanes]
                    acc = t if acc is None else acc + t
                out.append(acc)
            return out

        def finish(i):
            return [jnp.sum(wide[lax.rem(i, 2), q].T, axis=0, keepdims=True) for q in range(PER)]

        def put(i, sums):
            for q in range(PER):
                n = i * PER + q
                rowpart[n // 4, pl.ds(lax.rem(n, 4), 1), :] = sums[q]

        for q, part in enumerate(work(0)):
            wide[0, q] = part

        def body(i, _):
            sums = finish(i - 1)
            parts = work(i)
            put(i - 1, sums)
            for q in range(PER):
                wide[lax.rem(i, 2), q] = parts[q]
            return 0

        lax.fori_loop(1, NBLOCK, body, 0)
        put(NBLOCK - 1, finish(NBLOCK - 1))

    for step in range(ITERS):
        if step > 0:
            column_pass(step - 1)
        colbuf[step, pl.ds(y, 1)] = jnp.sum(colacc[...], axis=1)[None]
        exchange(lambda d: col_copy(step, d))
        colval[...] = 1.0 / (K * jnp.sum(colbuf[step], axis=0))
        row_pass()
        if step < ITERS - 1:
            rowbuf[step, pl.ds(me_p, 1)] = rowpart[pl.ds(4 * core, 4)][None]
            exchange(lambda d: rowp_copy(step, d))
            rowall[step, pl.ds(z, 1)] = jnp.sum(rowbuf[step], axis=0)[None]
            exchange(lambda d: rowz_copy(step, d))
            w = 1.0 / (IMAGES * jnp.sum(rowall[step], axis=0))
            for i in range(4):
                weight[step, core, 4 * i:4 * i + 4, :] = w[i]
            weight_copy(step).start()
            for d in range(1, 8):
                rowp_copy(step, d).wait_send()
        else:
            lastz[pl.ds(z, 1)] = rowpart[pl.ds(z, 1)]
            exchange(lastz_copy)
            lastp[pl.ds(me_p, 1)] = jnp.sum(lastz[...], axis=0)[None]
            exchange(lastp_copy)
            row_out[...] = jnp.log(IMAGES * (1.0 / (IMAGES * jnp.sum(lastp[...], axis=0))))
            col_out[...] = jnp.log(float(K) * float(IMAGES) * colval[pl.ds(y, 1), :])

    for r in range(2):
        for c in range(CHUNKS):
            def drain_ring(s, _):
                unit_copy(r, s, c).wait_send()
                piece_copy(r, s, c).wait_send()
                core_copy(r, s, c).wait_send()
                return 0

            lax.fori_loop(1, 5 - r, drain_ring, 0)
    for step in range(ITERS - 1):
        weight_copy(step).wait_send()

    def drain(d, _):
        for step in range(ITERS):
            col_copy(step, d).wait_send()
            if step < ITERS - 1:
                rowz_copy(step, d).wait_send()
        lastz_copy(d).wait_send()
        lastp_copy(d).wait_send()
        return 0

    lax.fori_loop(1, 8, drain, 0)


def local(features, prototypes):
    vmem = pl.BlockSpec(memory_space=pltpu.VMEM)
    row_log, col_log = pl.pallas_call(
        kernel,
        out_shape=(
            jax.ShapeDtypeStruct((ROWS // LANES, LANES), F32),
            jax.ShapeDtypeStruct((1, COLS), F32),
        ),
        in_specs=[vmem, vmem],
        out_specs=(vmem, vmem),
        scratch_shapes=[
            pltpu.VMEM((NY, NZ * ROWS, COLS), F32),
            pltpu.VMEM((NZ, ROWS, 256), BF16),
            pltpu.VMEM((NY, 256, COLS), BF16),
            pltpu.VMEM((NY, 1, COLS), F32),
            pltpu.VMEM((NY, 8, COLS), F32),
            pltpu.VMEM((ITERS, NY, NY, COLS), F32),
            pltpu.VMEM((NY, COLS), F32),
            pltpu.VMEM((NZ, 4, LANES), F32),
            pltpu.VMEM((ITERS - 1, NP, 4, 4, LANES), F32),
            pltpu.VMEM((ITERS - 1, NZ, 4, 4, LANES), F32),
            pltpu.VMEM((NZ, 4, LANES), F32),
            pltpu.VMEM((NP, 4, LANES), F32),
            pltpu.VMEM((ITERS - 1, 2, NZ * 2, LANES), F32),
            pltpu.VMEM((2, PER, LANES, LANES), F32),
        ]
        + [pltpu.SemaphoreType.DMA((2, 5, CHUNKS))] * 6
        + [pltpu.SemaphoreType.DMA((ITERS, 8))] * 6
        + [pltpu.SemaphoreType.DMA((ITERS - 1,))] * 2,
        compiler_params=pltpu.CompilerParams(
            collective_id=0, has_side_effects=True, vmem_limit_bytes=56 * 2**20
        ),
        cost_estimate=pl.CostEstimate(
            flops=2 * 4096 * 2048 * 256, bytes_accessed=2**20, transcendentals=4096 * 2048
        ),
        name="sinkhorn",
    )(features, prototypes)
    return row_log.reshape(ROWS), col_log.reshape(COLS)


def solution(mesh):
    in_specs = (P("dp", None), P(None, ("proto", "dp")))
    out_specs = (P("dp"), P(("proto", "dp")))
    return jax.shard_map(local, mesh=mesh, in_specs=in_specs, out_specs=out_specs, check_vma=False)
```

```python
import jax
import jax.numpy as jnp
from jax import lax
from jax.experimental import pallas as pl
from jax.experimental.pallas import tpu as pltpu
from jax.sharding import PartitionSpec as P

K = 131072
IMAGES = 32768
ITERS = 3
NY = 8
NZ = 8
NP = 8
ROWS = 512
COLS = 256
HALF = ROWS // 2
CHUNKS = 2
SPLIT = 4
PART = NZ // SPLIT
FAR_FIRST = (4, 3, 5, 2, 6, 1, 7)
BLOCK = 512
NBLOCK = NZ * ROWS // BLOCK
PER = BLOCK // 128
LANES = 128
EPS = 1e-6
LOG2E = 1.4426950408889634
SHARP = 0.07
F32 = jnp.float32
BF16 = jnp.bfloat16
MESH = pl.DeviceIdType.MESH


def near_first(k):
    return lax.rem(jnp.where(lax.rem(k, 2) == 1, (k + 1) // 2, 8 - k // 2), 8)


def kernel(
    feat, proto, row_out, col_out,
    tile, unit, piece, scale, colacc, colbuf, colval, rowpart, rowbuf, rowall, lastz, lastp, weight, wide,
    unit_send, unit_recv, core_send, core_recv, piece_send, piece_recv,
    col_send, col_recv, rowp_send, rowp_recv, rowz_send, rowz_recv,
):
    dp = lax.axis_index("dp")
    me_p = lax.axis_index("proto")
    y, z = dp // NZ, lax.rem(dp, NZ)
    core = lax.rem(me_p, 2)

    def y_peer(d):
        return (lax.rem(y + d, NY) * NZ + z, me_p)

    def z_peer(d):
        return (y * NZ + lax.rem(z + d, NZ), me_p)

    def p_peer(d):
        return (dp, lax.rem(me_p + d, NP))

    other_core = (dp, me_p + 1 - 2 * core)

    barrier = pltpu.get_barrier_semaphore()

    def greet(d, _):
        pl.semaphore_signal(barrier, inc=1, device_id=y_peer(d), device_id_type=MESH)
        pl.semaphore_signal(barrier, inc=1, device_id=z_peer(d), device_id_type=MESH)
        pl.semaphore_signal(barrier, inc=1, device_id=p_peer(d), device_id_type=MESH)
        return 0

    lax.fori_loop(1, 8, greet, 0)

    values = feat[...].astype(F32)
    norm = jnp.sqrt(jnp.sum(values * values, axis=1, keepdims=True) + EPS)
    unit[pl.ds(z, 1)] = (values / norm).astype(BF16)[None]
    piece[pl.ds(y, 1)] = proto[...][None]
    colacc[...] = jnp.zeros_like(colacc)

    def set_scale(vs):
        v = piece[vs].astype(F32)
        scale[vs] = (LOG2E / SHARP) / jnp.sqrt(jnp.sum(v * v, axis=0, keepdims=True) + EPS)

    set_scale(y)
    pl.semaphore_wait(barrier, 21)

    def chunk(c):
        return pl.ds(c * (256 // CHUNKS), 256 // CHUNKS)

    def half_chunk(c):
        rows = 256 // CHUNKS
        return pl.ds(pl.multiple_of(core * HALF + c * rows, rows), rows)

    def way(r):
        return 1 if r == 0 else 7

    def piece_copy(r, s, c):
        slot = lax.rem(y + 8 * (s - 1) - way(r) * (s - 1), NY)
        return pltpu.make_async_remote_copy(
            src_ref=piece.at[slot, chunk(c)], dst_ref=piece.at[slot, chunk(c)],
            send_sem=piece_send, recv_sem=piece_recv.at[r, s, c],
            device_id=y_peer(way(r)), device_id_type=MESH)

    def unit_copy(r, s, c):
        slot = lax.rem(z + 8 * (s - 1) - way(r) * (s - 1), NZ)
        return pltpu.make_async_remote_copy(
            src_ref=unit.at[slot, half_chunk(c)], dst_ref=unit.at[slot, half_chunk(c)],
            send_sem=unit_send, recv_sem=unit_recv.at[r, s, c],
            device_id=z_peer(way(r)), device_id_type=MESH)

    def core_copy(r, s, c):
        slot = lax.rem(z + 8 * s - way(r) * s, NZ)
        return pltpu.make_async_remote_copy(
            src_ref=unit.at[slot, half_chunk(c)], dst_ref=unit.at[slot, half_chunk(c)],
            send_sem=core_send, recv_sem=core_recv.at[r, s, c],
            device_id=other_core, device_id_type=MESH)

    for c in range(CHUNKS):
        for r in range(2):
            unit_copy(r, 1, c).start()
            piece_copy(r, 1, c).start()

    def slot_pair(t):
        k = sum((t >= j * j).astype(jnp.int32) for j in range(1, 8))
        rest = t - k * k
        ku = jnp.where(rest <= k, k, rest - k - 1)
        kv = jnp.where(rest <= k, rest, k)
        return lax.rem(z - near_first(ku) + NZ, NZ), lax.rem(y - near_first(kv) + NY, NY)

    def four(b, _):
        for q in range(4):
            us, vs = slot_pair(4 * b + q)
            e = jnp.exp2(jnp.dot(unit[us], piece[vs], preferred_element_type=F32) * scale[vs])
            tile[vs, pl.ds(pl.multiple_of(us * ROWS, ROWS), ROWS), :] = e
            colacc[vs] += jnp.sum(e.reshape(ROWS // 8, 8, COLS), axis=0)
        return 0

    def arrive(s, _):
        for c in range(CHUNKS):
            for r in range(2):
                @pl.when(s + r <= 4)
                def _():
                    unit_copy(r, s, c).wait_recv()
                    core_copy(r, s, c).start()

                    @pl.when(s + r < 4)
                    def _():
                        unit_copy(r, s + 1, c).start()

                    piece_copy(r, s, c).wait_recv()

                    @pl.when(s + r < 4)
                    def _():
                        piece_copy(r, s + 1, c).start()

        set_scale(lax.rem(y + 7 * s, NY))

        @pl.when(s < 4)
        def _():
            set_scale(lax.rem(y + s, NY))

        for c in range(CHUNKS):
            for r in range(2):
                @pl.when(s + r <= 4)
                def _():
                    core_copy(r, s, c).wait_recv()

        before = 2 * s - 1
        now = jnp.minimum(2 * s + 1, 8)
        lax.fori_loop(before * before // 4, now * now // 4, four, 0)
        return 0

    lax.fori_loop(1, 5, arrive, 0)

    def col_copy(step, d):
        return pltpu.make_async_remote_copy(
            src_ref=colbuf.at[step, 0], dst_ref=colbuf.at[step, d],
            send_sem=col_send.at[step], recv_sem=col_recv.at[step],
            device_id=y_peer(d), device_id_type=MESH)

    def rowp_copy(step, h, d):
        part = pl.ds(h * PART, PART)
        return pltpu.make_async_remote_copy(
            src_ref=rowpart.at[part], dst_ref=rowbuf.at[step, h, d],
            send_sem=rowp_send.at[step], recv_sem=rowp_recv.at[step, h],
            device_id=p_peer(d), device_id_type=MESH)

    def rowz_copy(step, h, d):
        return pltpu.make_async_remote_copy(
            src_ref=rowall.at[step, h, 0], dst_ref=rowall.at[step, h, d],
            send_sem=rowz_send.at[step], recv_sem=rowz_recv.at[step, h],
            device_id=z_peer(d), device_id_type=MESH)

    def lastz_copy(d):
        return pltpu.make_async_remote_copy(
            src_ref=rowpart.at[lax.rem(z + d, NZ)], dst_ref=lastz.at[d],
            send_sem=rowz_send.at[ITERS - 1], recv_sem=rowz_recv.at[ITERS - 1, 0],
            device_id=z_peer(d), device_id_type=MESH)

    def lastp_copy(d):
        return pltpu.make_async_remote_copy(
            src_ref=lastp.at[me_p], dst_ref=lastp.at[me_p],
            send_sem=rowp_send.at[ITERS - 1], recv_sem=rowp_recv.at[ITERS - 1, 0],
            device_id=p_peer(d), device_id_type=MESH)

    def settle(ref, semaphore):
        pltpu.make_async_copy(ref, ref, semaphore).wait()

    def send_all(copy):
        for d in FAR_FIRST:
            copy(d).start()

    def rows_of(i, q):
        return pl.ds(pl.multiple_of(i * BLOCK + q * LANES, LANES), LANES)

    def column_pass(step):
        def spread(i):
            return [jnp.broadcast_to(weight[i, q:q + 1, :], (LANES, LANES)).T for q in range(PER)]

        def part_pass(h, acc):
            settle(rowall.at[step, h, 1:], rowz_recv.at[step, h])
            weight[pl.ds(h * PART, PART)] = 1.0 / (IMAGES * jnp.sum(rowall[step, h], axis=0))
            first = h * PART
            for q, w in enumerate(spread(first)):
                wide[0, q] = w

            def body(i, acc):
                acc = list(acc)
                ws = [wide[lax.rem(i, 2), q] for q in range(PER)]
                ahead = spread(first + jnp.minimum(i + 1, PART - 1))
                for q in range(PER):
                    for j in range(2 * NY):
                        t = tile[j // 2, rows_of(first + i, q), (j % 2) * LANES:(j % 2 + 1) * LANES] * ws[q]
                        acc[j] = acc[j] + jnp.sum(t.reshape(LANES // 8, 8, LANES), axis=0)
                for q in range(PER):
                    wide[1 - lax.rem(i, 2), q] = ahead[q]
                return tuple(acc)

            return lax.fori_loop(0, PART, body, acc)

        acc = lax.fori_loop(0, SPLIT, part_pass, tuple(jnp.zeros((8, LANES), F32) for _ in range(2 * NY)))
        for j in range(2 * NY):
            colacc[j // 2, :, (j % 2) * LANES:(j % 2 + 1) * LANES] = acc[j]

    def row_pass(slot, done):
        def work(i):
            out = []
            for q in range(PER):
                acc = None
                for j in range(2 * NY):
                    lanes = slice((j % 2) * LANES, (j % 2 + 1) * LANES)
                    t = tile[j // 2, rows_of(slot(i), q), lanes] * colval[j // 2:j // 2 + 1, lanes]
                    acc = t if acc is None else acc + t
                out.append(acc)
            return out

        def finish(i):
            return [jnp.sum(wide[lax.rem(i, 2), q].T, axis=0, keepdims=True) for q in range(PER)]

        def put(i, sums):
            for q in range(PER):
                rowpart[slot(i), q:q + 1, :] = sums[q]

        for q, part in enumerate(work(0)):
            wide[0, q] = part

        def body(i, _):
            sums = finish(i - 1)
            parts = work(i)
            put(i - 1, sums)
            for q in range(PER):
                wide[lax.rem(i, 2), q] = parts[q]
            done(i - 1)
            return 0

        lax.fori_loop(1, NBLOCK, body, 0)
        put(NBLOCK - 1, finish(NBLOCK - 1))
        done(NBLOCK - 1)

    for step in range(ITERS):
        if step > 0:
            column_pass(step - 1)
        colbuf[step, 0] = jnp.sum(colacc[...], axis=1)
        send_all(lambda d: col_copy(step, d))
        settle(colbuf.at[step, 1:], col_recv.at[step])
        colval[...] = 1.0 / (K * jnp.sum(colbuf[step], axis=0))
        if step < ITERS - 1:
            def send_part(i):
                @pl.when(lax.rem(i, PART) == PART - 1)
                def _():
                    send_all(lambda d: rowp_copy(step, i // PART, d))

            row_pass(lambda i: i, send_part)

            def sum_part(h, _):
                settle(rowbuf.at[step, h, 1:], rowp_recv.at[step, h])
                rowall[step, h, 0] = rowpart[pl.ds(h * PART, PART)] + jnp.sum(rowbuf[step, h, 1:], axis=0)
                send_all(lambda d: rowz_copy(step, h, d))
                return 0

            lax.fori_loop(0, SPLIT, sum_part, 0)
            settle(rowbuf.at[step, :, 1:], rowp_send.at[step])
        else:
            def distance(i):
                return near_first(NBLOCK - 1 - i)

            def send_one(i):
                @pl.when(i < NBLOCK - 1)
                def _():
                    lastz_copy(distance(i)).start()

            row_pass(lambda i: lax.rem(z + distance(i), NZ), send_one)
            settle(lastz.at[1:], rowz_recv.at[ITERS - 1, 0])
            lastp[pl.ds(me_p, 1)] = rowpart[pl.ds(z, 1)] + jnp.sum(lastz[1:], axis=0)[None]
            send_all(lastp_copy)
            settle(lastp.at[1:], rowp_recv.at[ITERS - 1, 0])
            row_out[...] = IMAGES * (1.0 / (IMAGES * jnp.sum(lastp[...], axis=0)))
            col_out[...] = float(K) * float(IMAGES) * colval[pl.ds(y, 1), :]

    settle(unit.at[1:, pl.ds(0, HALF)], unit_send)
    settle(unit.at[1:, pl.ds(0, HALF)], core_send)
    settle(piece.at[1:], piece_send)
    for step in range(ITERS):
        settle(colbuf.at[step, 1:], col_send.at[step])
    for step in range(ITERS - 1):
        settle(rowall.at[step, :, 1:], rowz_send.at[step])
    settle(lastz.at[1:], rowz_send.at[ITERS - 1])
    settle(lastp.at[1:], rowp_send.at[ITERS - 1])


def local(features, prototypes):
    vmem = pl.BlockSpec(memory_space=pltpu.VMEM)
    row_mass, col_mass = pl.pallas_call(
        kernel,
        out_shape=(
            jax.ShapeDtypeStruct((ROWS // LANES, LANES), F32),
            jax.ShapeDtypeStruct((1, COLS), F32),
        ),
        in_specs=[vmem, vmem],
        out_specs=(vmem, vmem),
        scratch_shapes=[
            pltpu.VMEM((NY, NZ * ROWS, COLS), F32),
            pltpu.VMEM((NZ, ROWS, 256), BF16),
            pltpu.VMEM((NY, 256, COLS), BF16),
            pltpu.VMEM((NY, 1, COLS), F32),
            pltpu.VMEM((NY, 8, COLS), F32),
            pltpu.VMEM((ITERS, NY, NY, COLS), F32),
            pltpu.VMEM((NY, COLS), F32),
            pltpu.VMEM((NZ, 4, LANES), F32),
            pltpu.VMEM((ITERS - 1, SPLIT, NP, PART, 4, LANES), F32),
            pltpu.VMEM((ITERS - 1, SPLIT, NZ, PART, 4, LANES), F32),
            pltpu.VMEM((NZ, 4, LANES), F32),
            pltpu.VMEM((NP, 4, LANES), F32),
            pltpu.VMEM((NZ, 4, LANES), F32),
            pltpu.VMEM((2, PER, LANES, LANES), F32),
        ]
        + [pltpu.SemaphoreType.DMA, pltpu.SemaphoreType.DMA((2, 5, CHUNKS))] * 3
        + [pltpu.SemaphoreType.DMA((ITERS,))] * 2
        + [pltpu.SemaphoreType.DMA((ITERS,)), pltpu.SemaphoreType.DMA((ITERS, SPLIT))] * 2,
        compiler_params=pltpu.CompilerParams(
            collective_id=0, has_side_effects=True, vmem_limit_bytes=56 * 2**20
        ),
        cost_estimate=pl.CostEstimate(
            flops=2 * 4096 * 2048 * 256, bytes_accessed=2**20, transcendentals=4096 * 2048
        ),
        name="sinkhorn",
    )(features, prototypes)
    return jnp.log(row_mass.reshape(ROWS)), jnp.log(col_mass.reshape(COLS))


def solution(mesh):
    in_specs = (P("dp", None), P(None, ("proto", "dp")))
    out_specs = (P("dp"), P(("proto", "dp")))
    return jax.shard_map(local, mesh=mesh, in_specs=in_specs, out_specs=out_specs, check_vma=False)
```

```python
import jax
import jax.numpy as jnp
from jax import lax
from jax.experimental import pallas as pl
from jax.experimental.pallas import tpu as pltpu
from jax.sharding import PartitionSpec as P

K = 131072
IMAGES = 32768
ITERS = 3
NY = 8
NZ = 8
NP = 8
ROWS = 512
COLS = 256
HALF = ROWS // 2
CHUNKS = 2
GROUP = 8
SPLIT = 4
PART = NZ // SPLIT
FAR_FIRST = (4, 3, 5, 2, 6, 1, 7)
BLOCK = 512
NBLOCK = NZ * ROWS // BLOCK
PER = BLOCK // 128
LANES = 128
EPS = 1e-6
LOG2E = 1.4426950408889634
SHARP = 0.07
F32 = jnp.float32
BF16 = jnp.bfloat16
MESH = pl.DeviceIdType.MESH


def near_first(k):
    return lax.rem(jnp.where(lax.rem(k, 2) == 1, (k + 1) // 2, 8 - k // 2), 8)


def kernel(
    feat, proto, row_out, col_out,
    images, tile, unit, piece, scale, colacc, colbuf, colval, rowpart, rowbuf, rowall, lastz, lastp, weight, wide,
    in_sem, unit_send, unit_recv, core_send, core_recv, piece_send, piece_recv,
    col_send, col_recv, rowp_send, rowp_recv, rowz_send, rowz_recv,
):
    dp = lax.axis_index("dp")
    me_p = lax.axis_index("proto")
    y, z = dp // NZ, lax.rem(dp, NZ)
    core = lax.rem(me_p, 2)

    def y_peer(d):
        return (lax.rem(y + d, NY) * NZ + z, me_p)

    def z_peer(d):
        return (y * NZ + lax.rem(z + d, NZ), me_p)

    def p_peer(d):
        return (dp, lax.rem(me_p + d, NP))

    other_core = (dp, me_p + 1 - 2 * core)

    barrier = pltpu.get_barrier_semaphore()

    def greet(d, _):
        pl.semaphore_signal(barrier, inc=1, device_id=p_peer(d), device_id_type=MESH)
        return 0

    for d in (1, 7):
        pl.semaphore_signal(barrier, inc=1, device_id=y_peer(d), device_id_type=MESH)
        pl.semaphore_signal(barrier, inc=1, device_id=z_peer(d), device_id_type=MESH)
    lax.fori_loop(1, 8, greet, 0)

    def set_unit(rows):
        values = images[rows, :].astype(F32)
        norm = jnp.sqrt(jnp.sum(values * values, axis=1, keepdims=True) + EPS)
        unit[z, rows, :] = (values / norm).astype(BF16)

    def set_scale(vs):
        v = piece[vs].astype(F32)
        scale[vs] = (LOG2E / SHARP) / jnp.sqrt(jnp.sum(v * v, axis=0, keepdims=True) + EPS)

    proto_copy = pltpu.make_async_copy(proto, piece.at[y], in_sem.at[0])
    feat_copy = pltpu.make_async_copy(feat, images, in_sem.at[1])
    proto_copy.start()
    feat_copy.start()
    proto_copy.wait()
    pl.semaphore_wait(barrier, 11)

    def chunk(c):
        return pl.ds(c * (256 // CHUNKS), 256 // CHUNKS)

    def half_chunk(c):
        rows = 256 // CHUNKS
        return pl.ds(pl.multiple_of(core * HALF + c * rows, rows), rows)

    def way(r):
        return 1 if r == 0 else 7

    def piece_copy(r, s, c):
        slot = lax.rem(y + 8 * (s - 1) - way(r) * (s - 1), NY)
        return pltpu.make_async_remote_copy(
            src_ref=piece.at[slot, chunk(c)], dst_ref=piece.at[slot, chunk(c)],
            send_sem=piece_send, recv_sem=piece_recv.at[r, s, c],
            device_id=y_peer(way(r)), device_id_type=MESH)

    def unit_copy(r, s, c):
        slot = lax.rem(z + 8 * (s - 1) - way(r) * (s - 1), NZ)
        return pltpu.make_async_remote_copy(
            src_ref=unit.at[slot, half_chunk(c)], dst_ref=unit.at[slot, half_chunk(c)],
            send_sem=unit_send, recv_sem=unit_recv.at[r, s, c],
            device_id=z_peer(way(r)), device_id_type=MESH)

    def core_copy(r, s, c):
        slot = lax.rem(z + 8 * s - way(r) * s, NZ)
        return pltpu.make_async_remote_copy(
            src_ref=unit.at[slot, half_chunk(c)], dst_ref=unit.at[slot, half_chunk(c)],
            send_sem=core_send, recv_sem=core_recv.at[r, s, c],
            device_id=other_core, device_id_type=MESH)

    for c in range(CHUNKS):
        for r in range(2):
            piece_copy(r, 1, c).start()
    feat_copy.wait()
    set_unit(pl.ds(pl.multiple_of(core * HALF, HALF), HALF))
    for c in range(CHUNKS):
        for r in range(2):
            unit_copy(r, 1, c).start()
    set_unit(pl.ds(pl.multiple_of((1 - core) * HALF, HALF), HALF))
    set_scale(y)
    colacc[...] = jnp.zeros_like(colacc)
    wide[...] = jnp.zeros_like(wide)

    def slot_pair(t):
        k = sum((t >= j * j).astype(jnp.int32) for j in range(1, 8))
        rest = t - k * k
        ku = jnp.where(rest < k, rest, k)
        kv = jnp.where(rest < k, k, rest - k)
        return lax.rem(z - near_first(ku) + NZ, NZ), lax.rem(y - near_first(kv) + NY, NY)

    def blocks(b, _):
        for q in range(GROUP):
            us, vs = slot_pair(GROUP * b + q)
            e = jnp.exp2(jnp.dot(unit[us], piece[vs], preferred_element_type=F32) * scale[vs])
            tile[vs, pl.ds(pl.multiple_of(us * ROWS, ROWS), ROWS), :] = e
            colacc[vs] += jnp.sum(e.reshape(ROWS // 8, 8, COLS), axis=0)
        return 0

    def last_block(s):
        return s + (s >= 2).astype(jnp.int32) + 2 * (s >= 3).astype(jnp.int32)

    def arrive(s, _):
        for c in range(CHUNKS):
            for r in range(2):
                for copy in (piece_copy, unit_copy):
                    @pl.when(s + r <= 4)
                    def _():
                        copy(r, s, c).wait_recv()

                        @pl.when(s + r < 4)
                        def _():
                            copy(r, s + 1, c).start()

            for r in range(2):
                @pl.when(s + r <= 4)
                def _():
                    core_copy(r, s, c).start()

        @pl.when(s <= 4)
        def _():
            set_scale(lax.rem(y + 7 * s, NY))

        @pl.when(s < 4)
        def _():
            set_scale(lax.rem(y + s, NY))
            for c in range(CHUNKS):
                for r in range(2):
                    core_copy(r, s, c).wait_recv()

        @pl.when(s == 5)
        def _():
            for c in range(CHUNKS):
                core_copy(0, 4, c).wait_recv()

        lax.fori_loop(last_block(s - 1), last_block(s), blocks, 0)
        return 0

    lax.fori_loop(1, 6, arrive, 0)

    def col_copy(step, d):
        return pltpu.make_async_remote_copy(
            src_ref=colbuf.at[step, 0], dst_ref=colbuf.at[step, d],
            send_sem=col_send.at[step], recv_sem=col_recv.at[step],
            device_id=y_peer(d), device_id_type=MESH)

    def rowp_copy(step, h, d):
        part = pl.ds(h * PART, PART)
        return pltpu.make_async_remote_copy(
            src_ref=rowpart.at[part], dst_ref=rowbuf.at[step, h, d],
            send_sem=rowp_send.at[step], recv_sem=rowp_recv.at[step, h],
            device_id=p_peer(d), device_id_type=MESH)

    def rowz_copy(step, h, d):
        return pltpu.make_async_remote_copy(
            src_ref=rowall.at[step, h, 0], dst_ref=rowall.at[step, h, d],
            send_sem=rowz_send.at[step], recv_sem=rowz_recv.at[step, h],
            device_id=z_peer(d), device_id_type=MESH)

    def lastz_copy(d):
        return pltpu.make_async_remote_copy(
            src_ref=rowpart.at[lax.rem(z + d, NZ)], dst_ref=lastz.at[d],
            send_sem=rowz_send.at[ITERS - 1], recv_sem=rowz_recv.at[ITERS - 1, 0],
            device_id=z_peer(d), device_id_type=MESH)

    def lastp_copy(d):
        return pltpu.make_async_remote_copy(
            src_ref=lastp.at[me_p], dst_ref=lastp.at[me_p],
            send_sem=rowp_send.at[ITERS - 1], recv_sem=rowp_recv.at[ITERS - 1, 0],
            device_id=p_peer(d), device_id_type=MESH)

    def settle(ref, semaphore):
        pltpu.make_async_copy(ref, ref, semaphore).wait()

    def send_all(copy):
        for d in FAR_FIRST:
            copy(d).start()

    def rows_of(i, q):
        return pl.ds(pl.multiple_of(i * BLOCK + q * LANES, LANES), LANES)

    def column_pass(step):
        def spread(i):
            return [jnp.broadcast_to(weight[i, q:q + 1, :], (LANES, LANES)).T for q in range(PER)]

        def part_pass(h, acc):
            settle(rowall.at[step, h, 1:], rowz_recv.at[step, h])
            weight[pl.ds(h * PART, PART)] = 1.0 / (IMAGES * jnp.sum(rowall[step, h], axis=0))
            first = h * PART
            for q, w in enumerate(spread(first)):
                wide[0, q] = w

            def body(i, acc):
                acc = list(acc)
                ws = [wide[lax.rem(i, 2), q] for q in range(PER)]
                ahead = spread(first + jnp.minimum(i + 1, PART - 1))
                for q in range(PER):
                    for j in range(2 * NY):
                        t = tile[j // 2, rows_of(first + i, q), (j % 2) * LANES:(j % 2 + 1) * LANES] * ws[q]
                        acc[j] = acc[j] + jnp.sum(t.reshape(LANES // 8, 8, LANES), axis=0)
                for q in range(PER):
                    wide[1 - lax.rem(i, 2), q] = ahead[q]
                return tuple(acc)

            return lax.fori_loop(0, PART, body, acc)

        acc = lax.fori_loop(0, SPLIT, part_pass, tuple(jnp.zeros((8, LANES), F32) for _ in range(2 * NY)))
        for j in range(2 * NY):
            colacc[j // 2, :, (j % 2) * LANES:(j % 2 + 1) * LANES] = acc[j]

    def row_pass(slot, done):
        def work(i):
            out = []
            for q in range(PER):
                acc = None
                for j in range(2 * NY):
                    lanes = slice((j % 2) * LANES, (j % 2 + 1) * LANES)
                    t = tile[j // 2, rows_of(slot(i), q), lanes] * colval[j // 2:j // 2 + 1, lanes]
                    acc = t if acc is None else acc + t
                out.append(acc)
            return out

        def finish(i):
            return [jnp.sum(wide[lax.rem(i, 2), q].T, axis=0, keepdims=True) for q in range(PER)]

        def put(i, sums):
            for q in range(PER):
                rowpart[slot(i), q:q + 1, :] = sums[q]

        def store(i, parts):
            for q in range(PER):
                wide[lax.rem(i, 2), q] = parts[q]

        def body(i, _):
            before = jnp.maximum(i - 1, 0)
            sums = finish(i + 1)
            parts = work(i)
            put(before, sums)
            store(i, parts)

            @pl.when((i > 0) & (lax.rem(i, PART) == 0))
            def _():
                done(i // PART - 1)

            return 0

        lax.fori_loop(0, NBLOCK, body, 0)
        put(NBLOCK - 1, finish(NBLOCK - 1))
        done(SPLIT - 1)

    def distance(i):
        return near_first(NBLOCK - 1 - i)

    def iteration(step, _):
        last = step == ITERS - 1

        @pl.when(step > 0)
        def _():
            column_pass(step - 1)

        colbuf[step, 0] = jnp.sum(colacc[...], axis=1)
        send_all(lambda d: col_copy(step, d))
        settle(colbuf.at[step, 1:], col_recv.at[step])
        colval[...] = 1.0 / (K * jnp.sum(colbuf[step], axis=0))

        def send_part(h):
            @pl.when(jnp.logical_not(last))
            def _():
                send_all(lambda d: rowp_copy(step, h, d))

            @pl.when(last)
            def _():
                lastz_copy(distance(2 * h)).start()

                @pl.when(h < SPLIT - 1)
                def _():
                    lastz_copy(distance(2 * h + 1)).start()

        row_pass(lambda i: jnp.where(last, lax.rem(z + distance(i), NZ), i), send_part)

        @pl.when(jnp.logical_not(last))
        def _():
            def sum_part(h, _):
                settle(rowbuf.at[step, h, 1:], rowp_recv.at[step, h])
                rowall[step, h, 0] = rowpart[pl.ds(h * PART, PART)] + jnp.sum(rowbuf[step, h, 1:], axis=0)
                send_all(lambda d: rowz_copy(step, h, d))
                return 0

            lax.fori_loop(0, SPLIT, sum_part, 0)
            settle(rowbuf.at[step, :, 1:], rowp_send.at[step])

        return 0

    lax.fori_loop(0, ITERS, iteration, 0)
    settle(lastz.at[1:], rowz_recv.at[ITERS - 1, 0])
    lastp[pl.ds(me_p, 1)] = rowpart[pl.ds(z, 1)] + jnp.sum(lastz[1:], axis=0)[None]
    send_all(lastp_copy)
    settle(lastp.at[1:], rowp_recv.at[ITERS - 1, 0])
    row_out[...] = IMAGES * (1.0 / (IMAGES * jnp.sum(lastp[...], axis=0)))
    col_out[...] = float(K) * float(IMAGES) * colval[pl.ds(y, 1), :]

    settle(unit.at[1:, pl.ds(0, HALF)], unit_send)
    settle(unit.at[1:, pl.ds(0, HALF)], core_send)
    settle(piece.at[1:], piece_send)
    for step in range(ITERS):
        settle(colbuf.at[step, 1:], col_send.at[step])
    for step in range(ITERS - 1):
        settle(rowall.at[step, :, 1:], rowz_send.at[step])
    settle(lastz.at[1:], rowz_send.at[ITERS - 1])
    settle(lastp.at[1:], rowp_send.at[ITERS - 1])


def local(features, prototypes):
    vmem = pl.BlockSpec(memory_space=pltpu.VMEM)
    row_mass, col_mass = pl.pallas_call(
        kernel,
        out_shape=(
            jax.ShapeDtypeStruct((ROWS // LANES, LANES), F32),
            jax.ShapeDtypeStruct((1, COLS), F32),
        ),
        in_specs=[pl.BlockSpec(memory_space=pltpu.HBM)] * 2,
        out_specs=(vmem, vmem),
        scratch_shapes=[
            pltpu.VMEM((ROWS, 256), BF16),
            pltpu.VMEM((NY, NZ * ROWS, COLS), F32),
            pltpu.VMEM((NZ, ROWS, 256), BF16),
            pltpu.VMEM((NY, 256, COLS), BF16),
            pltpu.VMEM((NY, 1, COLS), F32),
            pltpu.VMEM((NY, 8, COLS), F32),
            pltpu.VMEM((ITERS, NY, NY, COLS), F32),
            pltpu.VMEM((NY, COLS), F32),
            pltpu.VMEM((NZ, 4, LANES), F32),
            pltpu.VMEM((ITERS - 1, SPLIT, NP, PART, 4, LANES), F32),
            pltpu.VMEM((ITERS - 1, SPLIT, NZ, PART, 4, LANES), F32),
            pltpu.VMEM((NZ, 4, LANES), F32),
            pltpu.VMEM((NP, 4, LANES), F32),
            pltpu.VMEM((NZ, 4, LANES), F32),
            pltpu.VMEM((2, PER, LANES, LANES), F32),
        ]
        + [pltpu.SemaphoreType.DMA((2,))]
        + [pltpu.SemaphoreType.DMA, pltpu.SemaphoreType.DMA((2, 5, CHUNKS))] * 3
        + [pltpu.SemaphoreType.DMA((ITERS,))] * 2
        + [pltpu.SemaphoreType.DMA((ITERS,)), pltpu.SemaphoreType.DMA((ITERS, SPLIT))] * 2,
        compiler_params=pltpu.CompilerParams(
            collective_id=0, has_side_effects=True, vmem_limit_bytes=40 * 2**20
        ),
        cost_estimate=pl.CostEstimate(
            flops=2 * 4096 * 2048 * 256, bytes_accessed=2**20, transcendentals=4096 * 2048
        ),
        name="sinkhorn",
    )(features, prototypes)
    return jnp.log(row_mass.reshape(ROWS)), jnp.log(col_mass.reshape(COLS))


def solution(mesh):
    in_specs = (P("dp", None), P(None, ("proto", "dp")))
    out_specs = (P("dp"), P(("proto", "dp")))
    return jax.shard_map(local, mesh=mesh, in_specs=in_specs, out_specs=out_specs, check_vma=False)
```

```python
import jax
import jax.numpy as jnp
from jax import lax
from jax.experimental import pallas as pl
from jax.experimental.pallas import tpu as pltpu
from jax.sharding import PartitionSpec as P

K = 131072
IMAGES = 32768
ITERS = 3
NY = 8
NZ = 8
NP = 8
ROWS = 512
COLS = 256
HALF = ROWS // 2
CHUNKS = 2
GROUP = 8
SPLIT = 4
PART = NZ // SPLIT
FAR_FIRST = (4, 3, 5, 2, 6, 1, 7)
BLOCK = 512
NBLOCK = NZ * ROWS // BLOCK
PER = BLOCK // 128
LANES = 128
EPS = 1e-6
LOG2E = 1.4426950408889634
SHARP = 0.07
F32 = jnp.float32
BF16 = jnp.bfloat16
MESH = pl.DeviceIdType.MESH


def near_first(k):
    return lax.rem(jnp.where(lax.rem(k, 2) == 1, (k + 1) // 2, 8 - k // 2), 8)


def kernel(
    feat, proto, row_out, col_out,
    images, tile, unit, piece, scale, colacc, colbuf, colval, rowpart, rowbuf, rowall, lastz, lastp, weight, wide,
    in_sem, unit_send, unit_recv, core_send, core_recv, piece_send, piece_recv,
    col_send, col_recv, rowp_send, rowp_recv, rowz_send, rowz_recv,
):
    dp = lax.axis_index("dp")
    me_p = lax.axis_index("proto")
    y, z = dp // NZ, lax.rem(dp, NZ)
    core = lax.rem(me_p, 2)

    def y_peer(d):
        return (lax.rem(y + d, NY) * NZ + z, me_p)

    def z_peer(d):
        return (y * NZ + lax.rem(z + d, NZ), me_p)

    def p_peer(d):
        return (dp, lax.rem(me_p + d, NP))

    other_core = (dp, me_p + 1 - 2 * core)

    barrier = pltpu.get_barrier_semaphore()

    def greet(d, _):
        pl.semaphore_signal(barrier, inc=1, device_id=p_peer(d), device_id_type=MESH)
        return 0

    for d in (1, 7):
        pl.semaphore_signal(barrier, inc=1, device_id=y_peer(d), device_id_type=MESH)
        pl.semaphore_signal(barrier, inc=1, device_id=z_peer(d), device_id_type=MESH)
    lax.fori_loop(1, 8, greet, 0)

    def set_unit(rows):
        values = images[rows, :].astype(F32)
        norm = jnp.sqrt(jnp.sum(values * values, axis=1, keepdims=True) + EPS)
        unit[z, rows, :] = (values / norm).astype(BF16)

    def set_scale(vs):
        v = piece[vs].astype(F32)
        scale[vs] = (LOG2E / SHARP) / jnp.sqrt(jnp.sum(v * v, axis=0, keepdims=True) + EPS)

    proto_copy = pltpu.make_async_copy(proto, piece.at[y], in_sem.at[0])
    feat_copy = pltpu.make_async_copy(feat, images, in_sem.at[1])
    proto_copy.start()
    feat_copy.start()
    proto_copy.wait()
    pl.semaphore_wait(barrier, 11)

    def chunk(c):
        return pl.ds(c * (256 // CHUNKS), 256 // CHUNKS)

    def half_chunk(c):
        rows = 256 // CHUNKS
        return pl.ds(pl.multiple_of(core * HALF + c * rows, rows), rows)

    def way(r):
        return 1 if r == 0 else 7

    def piece_copy(r, s, c):
        slot = lax.rem(y + 8 * (s - 1) - way(r) * (s - 1), NY)
        return pltpu.make_async_remote_copy(
            src_ref=piece.at[slot, chunk(c)], dst_ref=piece.at[slot, chunk(c)],
            send_sem=piece_send, recv_sem=piece_recv.at[r, s, c],
            device_id=y_peer(way(r)), device_id_type=MESH)

    def unit_copy(r, s, c):
        slot = lax.rem(z + 8 * (s - 1) - way(r) * (s - 1), NZ)
        return pltpu.make_async_remote_copy(
            src_ref=unit.at[slot, half_chunk(c)], dst_ref=unit.at[slot, half_chunk(c)],
            send_sem=unit_send, recv_sem=unit_recv.at[r, s, c],
            device_id=z_peer(way(r)), device_id_type=MESH)

    def core_copy(r, s, c):
        slot = lax.rem(z + 8 * s - way(r) * s, NZ)
        return pltpu.make_async_remote_copy(
            src_ref=unit.at[slot, half_chunk(c)], dst_ref=unit.at[slot, half_chunk(c)],
            send_sem=core_send, recv_sem=core_recv.at[r, s, c],
            device_id=other_core, device_id_type=MESH)

    for c in range(CHUNKS):
        for r in range(2):
            piece_copy(r, 1, c).start()
    feat_copy.wait()
    set_unit(pl.ds(pl.multiple_of(core * HALF, HALF), HALF))
    for c in range(CHUNKS):
        for r in range(2):
            unit_copy(r, 1, c).start()
    set_unit(pl.ds(pl.multiple_of((1 - core) * HALF, HALF), HALF))
    set_scale(y)
    colacc[...] = jnp.zeros_like(colacc)
    wide[...] = jnp.zeros_like(wide)

    def slot_pair(t):
        k = sum((t >= j * j).astype(jnp.int32) for j in range(1, 8))
        rest = t - k * k
        ku = jnp.where(rest < k, rest, k)
        kv = jnp.where(rest < k, k, rest - k)
        return lax.rem(z - near_first(ku) + NZ, NZ), lax.rem(y - near_first(kv) + NY, NY)

    def blocks(b, _):
        for q in range(GROUP):
            us, vs = slot_pair(GROUP * b + q)
            e = jnp.exp2(jnp.dot(unit[us], piece[vs], preferred_element_type=F32) * scale[vs])
            tile[vs, pl.ds(pl.multiple_of(us * ROWS, ROWS), ROWS), :] = e
            colacc[vs] += jnp.sum(e.reshape(ROWS // 8, 8, COLS), axis=0)
        return 0

    def last_block(s):
        return s + (s >= 2).astype(jnp.int32) + 2 * (s >= 3).astype(jnp.int32)

    def arrive(s, _):
        for c in range(CHUNKS):
            for r in range(2):
                for copy in (piece_copy, unit_copy):
                    @pl.when(s + r <= 4)
                    def _():
                        copy(r, s, c).wait_recv()

                        @pl.when(s + r < 4)
                        def _():
                            copy(r, s + 1, c).start()

            for r in range(2):
                @pl.when(s + r <= 4)
                def _():
                    core_copy(r, s, c).start()

        @pl.when(s <= 4)
        def _():
            set_scale(lax.rem(y + 7 * s, NY))

        @pl.when(s < 4)
        def _():
            set_scale(lax.rem(y + s, NY))
            for c in range(CHUNKS):
                for r in range(2):
                    core_copy(r, s, c).wait_recv()

        @pl.when(s == 5)
        def _():
            for c in range(CHUNKS):
                core_copy(0, 4, c).wait_recv()

        lax.fori_loop(last_block(s - 1), last_block(s), blocks, 0)
        return 0

    lax.fori_loop(1, 6, arrive, 0)

    def col_copy(step, d):
        return pltpu.make_async_remote_copy(
            src_ref=colbuf.at[step, 0], dst_ref=colbuf.at[step, d],
            send_sem=col_send.at[step], recv_sem=col_recv.at[step],
            device_id=y_peer(d), device_id_type=MESH)

    def rowp_copy(step, h, d):
        part = pl.ds(h * PART, PART)
        return pltpu.make_async_remote_copy(
            src_ref=rowpart.at[part], dst_ref=rowbuf.at[step, h, d],
            send_sem=rowp_send.at[step], recv_sem=rowp_recv.at[step, h],
            device_id=p_peer(d), device_id_type=MESH)

    def rowz_copy(step, h, d):
        return pltpu.make_async_remote_copy(
            src_ref=rowall.at[step, h, 0], dst_ref=rowall.at[step, h, d],
            send_sem=rowz_send.at[step], recv_sem=rowz_recv.at[step, h],
            device_id=z_peer(d), device_id_type=MESH)

    def lastz_copy(d):
        return pltpu.make_async_remote_copy(
            src_ref=rowpart.at[lax.rem(z + d, NZ)], dst_ref=lastz.at[d],
            send_sem=rowz_send.at[ITERS - 1], recv_sem=rowz_recv.at[ITERS - 1, 0],
            device_id=z_peer(d), device_id_type=MESH)

    def lastp_copy(d):
        return pltpu.make_async_remote_copy(
            src_ref=lastp.at[me_p], dst_ref=lastp.at[me_p],
            send_sem=rowp_send.at[ITERS - 1], recv_sem=rowp_recv.at[ITERS - 1, 0],
            device_id=p_peer(d), device_id_type=MESH)

    def settle(ref, semaphore):
        pltpu.make_async_copy(ref, ref, semaphore).wait()

    def send_all(copy):
        for d in FAR_FIRST:
            copy(d).start()

    def rows_of(i, q):
        return pl.ds(pl.multiple_of(i * BLOCK + q * LANES, LANES), LANES)

    def column_pass(step):
        def spread(i):
            return [jnp.broadcast_to(weight[i, q:q + 1, :], (LANES, LANES)).T for q in range(PER)]

        def part_pass(h, acc):
            settle(rowall.at[step, h, 1:], rowz_recv.at[step, h])
            weight[pl.ds(h * PART, PART)] = 1.0 / (IMAGES * jnp.sum(rowall[step, h], axis=0))
            first = h * PART
            for q, w in enumerate(spread(first)):
                wide[0, q] = w

            def body(i, acc):
                acc = list(acc)
                ws = [wide[lax.rem(i, 2), q] for q in range(PER)]
                ahead = spread(first + jnp.minimum(i + 1, PART - 1))
                for q in range(PER):
                    for j in range(2 * NY):
                        t = tile[j // 2, rows_of(first + i, q), (j % 2) * LANES:(j % 2 + 1) * LANES] * ws[q]
                        acc[j] = acc[j] + jnp.sum(t.reshape(LANES // 8, 8, LANES), axis=0)
                for q in range(PER):
                    wide[1 - lax.rem(i, 2), q] = ahead[q]
                return tuple(acc)

            return lax.fori_loop(0, PART, body, acc)

        acc = lax.fori_loop(0, SPLIT, part_pass, tuple(jnp.zeros((8, LANES), F32) for _ in range(2 * NY)))
        for j in range(2 * NY):
            colacc[j // 2, :, (j % 2) * LANES:(j % 2 + 1) * LANES] = acc[j]

    def row_pass(slot, done):
        def work(i):
            out = []
            for q in range(PER):
                acc = None
                for j in range(2 * NY):
                    lanes = slice((j % 2) * LANES, (j % 2 + 1) * LANES)
                    t = tile[j // 2, rows_of(slot(i), q), lanes] * colval[j // 2:j // 2 + 1, lanes]
                    acc = t if acc is None else acc + t
                out.append(acc)
            return out

        def finish(i):
            return [jnp.sum(wide[lax.rem(i, 2), q].T, axis=0, keepdims=True) for q in range(PER)]

        def put(i, sums):
            for q in range(PER):
                rowpart[slot(i), q:q + 1, :] = sums[q]

        def store(i, parts):
            for q in range(PER):
                wide[lax.rem(i, 2), q] = parts[q]

        def body(i, _):
            before = jnp.maximum(i - 1, 0)
            sums = finish(i + 1)
            parts = work(i)
            put(before, sums)
            store(i, parts)

            @pl.when((i > 0) & (lax.rem(i, PART) == 0))
            def _():
                done(i // PART - 1)

            return 0

        lax.fori_loop(0, NBLOCK, body, 0)
        put(NBLOCK - 1, finish(NBLOCK - 1))
        done(SPLIT - 1)

    def distance(i):
        return near_first(NBLOCK - 1 - i)

    def iteration(step, _):
        last = step == ITERS - 1

        @pl.when(step > 0)
        def _():
            column_pass(step - 1)

        colbuf[step, 0] = jnp.sum(colacc[...], axis=1)
        send_all(lambda d: col_copy(step, d))
        settle(colbuf.at[step, 1:], col_recv.at[step])
        colval[...] = 1.0 / (K * jnp.sum(colbuf[step], axis=0))

        def send_part(h):
            @pl.when(jnp.logical_not(last))
            def _():
                send_all(lambda d: rowp_copy(step, h, d))

            @pl.when(last)
            def _():
                lastz_copy(distance(2 * h)).start()

                @pl.when(h < SPLIT - 1)
                def _():
                    lastz_copy(distance(2 * h + 1)).start()

        row_pass(lambda i: jnp.where(last, lax.rem(z + distance(i), NZ), i), send_part)

        @pl.when(jnp.logical_not(last))
        def _():
            def sum_part(h, _):
                settle(rowbuf.at[step, h, 1:], rowp_recv.at[step, h])
                rowall[step, h, 0] = rowpart[pl.ds(h * PART, PART)] + jnp.sum(rowbuf[step, h, 1:], axis=0)
                send_all(lambda d: rowz_copy(step, h, d))
                return 0

            lax.fori_loop(0, SPLIT, sum_part, 0)
            settle(rowbuf.at[step, :, 1:], rowp_send.at[step])

        return 0

    lax.fori_loop(0, ITERS, iteration, 0)
    settle(lastz.at[1:], rowz_recv.at[ITERS - 1, 0])
    lastp[pl.ds(me_p, 1)] = rowpart[pl.ds(z, 1)] + jnp.sum(lastz[1:], axis=0)[None]
    send_all(lastp_copy)
    settle(lastp.at[1:], rowp_recv.at[ITERS - 1, 0])
    row_out[...] = IMAGES * (1.0 / (IMAGES * jnp.sum(lastp[...], axis=0)))
    col_out[...] = float(K) * float(IMAGES) * colval[pl.ds(y, 1), :]

    settle(unit.at[1:, pl.ds(0, HALF)], unit_send)
    settle(unit.at[1:, pl.ds(0, HALF)], core_send)
    settle(piece.at[1:], piece_send)
    for step in range(ITERS):
        settle(colbuf.at[step, 1:], col_send.at[step])
    for step in range(ITERS - 1):
        settle(rowall.at[step, :, 1:], rowz_send.at[step])
    settle(lastz.at[1:], rowz_send.at[ITERS - 1])
    settle(lastp.at[1:], rowp_send.at[ITERS - 1])


def logs(row_mass, col_mass, row_log, col_log):
    row_log[...] = jnp.log(row_mass[...])
    col_log[...] = jnp.log(col_mass[...])


def local(features, prototypes):
    vmem = pl.BlockSpec(memory_space=pltpu.VMEM)
    row_mass, col_mass = pl.pallas_call(
        kernel,
        out_shape=(
            jax.ShapeDtypeStruct((ROWS // LANES, LANES), F32),
            jax.ShapeDtypeStruct((1, COLS), F32),
        ),
        in_specs=[pl.BlockSpec(memory_space=pltpu.HBM)] * 2,
        out_specs=(vmem, vmem),
        scratch_shapes=[
            pltpu.VMEM((ROWS, 256), BF16),
            pltpu.VMEM((NY, NZ * ROWS, COLS), F32),
            pltpu.VMEM((NZ, ROWS, 256), BF16),
            pltpu.VMEM((NY, 256, COLS), BF16),
            pltpu.VMEM((NY, 1, COLS), F32),
            pltpu.VMEM((NY, 8, COLS), F32),
            pltpu.VMEM((ITERS, NY, NY, COLS), F32),
            pltpu.VMEM((NY, COLS), F32),
            pltpu.VMEM((NZ, 4, LANES), F32),
            pltpu.VMEM((ITERS - 1, SPLIT, NP, PART, 4, LANES), F32),
            pltpu.VMEM((ITERS - 1, SPLIT, NZ, PART, 4, LANES), F32),
            pltpu.VMEM((NZ, 4, LANES), F32),
            pltpu.VMEM((NP, 4, LANES), F32),
            pltpu.VMEM((NZ, 4, LANES), F32),
            pltpu.VMEM((2, PER, LANES, LANES), F32),
        ]
        + [pltpu.SemaphoreType.DMA((2,))]
        + [pltpu.SemaphoreType.DMA, pltpu.SemaphoreType.DMA((2, 5, CHUNKS))] * 3
        + [pltpu.SemaphoreType.DMA((ITERS,))] * 2
        + [pltpu.SemaphoreType.DMA((ITERS,)), pltpu.SemaphoreType.DMA((ITERS, SPLIT))] * 2,
        compiler_params=pltpu.CompilerParams(
            collective_id=0, has_side_effects=True, vmem_limit_bytes=56 * 2**20
        ),
        cost_estimate=pl.CostEstimate(
            flops=2 * 4096 * 2048 * 256, bytes_accessed=2**20, transcendentals=4096 * 2048
        ),
        name="sinkhorn",
    )(features, prototypes)
    row_log, col_log = pl.pallas_call(
        logs,
        out_shape=(
            jax.ShapeDtypeStruct((ROWS // LANES, LANES), F32),
            jax.ShapeDtypeStruct((1, COLS), F32),
        ),
        in_specs=[vmem, vmem],
        out_specs=(vmem, vmem),
        name="logs",
    )(row_mass, col_mass)
    return row_log.reshape(ROWS), col_log.reshape(COLS)


def solution(mesh):
    in_specs = (P("dp", None), P(None, ("proto", "dp")))
    out_specs = (P("dp"), P(("proto", "dp")))
    return jax.shard_map(local, mesh=mesh, in_specs=in_specs, out_specs=out_specs, check_vma=False)
```

```python
import jax
import jax.numpy as jnp
from jax import lax
from jax.experimental import pallas as pl
from jax.experimental.pallas import tpu as pltpu
from jax.sharding import PartitionSpec as P

K = 131072
IMAGES = 32768
ITERS = 3
NY = 8
NZ = 8
NP = 8
ROWS = 512
COLS = 256
HALF = ROWS // 2
CHUNKS = 2
GROUP = 8
SPLIT = 8
PART = NZ // SPLIT
FAR_FIRST = (4, 3, 5, 2, 6, 1, 7)
BLOCK = 512
NBLOCK = NZ * ROWS // BLOCK
PER = BLOCK // 128
LANES = 128
EPS = 1e-6
LOG2E = 1.4426950408889634
SHARP = 0.07
F32 = jnp.float32
BF16 = jnp.bfloat16
MESH = pl.DeviceIdType.MESH


def near_first(k):
    return lax.rem(jnp.where(lax.rem(k, 2) == 1, (k + 1) // 2, 8 - k // 2), 8)


def kernel(
    feat, proto, row_out, col_out,
    images, tile, unit, piece, scale, colacc, colbuf, colval, rowpart, rowbuf, rowall, lastz, lastp, weight, wide,
    in_sem, unit_send, unit_recv, core_send, core_recv, piece_send, piece_recv,
    col_send, col_recv, rowp_send, rowp_recv, rowz_send, rowz_recv,
):
    dp = lax.axis_index("dp")
    me_p = lax.axis_index("proto")
    y, z = dp // NZ, lax.rem(dp, NZ)
    core = lax.rem(me_p, 2)

    def y_peer(d):
        return (lax.rem(y + d, NY) * NZ + z, me_p)

    def z_peer(d):
        return (y * NZ + lax.rem(z + d, NZ), me_p)

    def p_peer(d):
        return (dp, lax.rem(me_p + d, NP))

    other_core = (dp, me_p + 1 - 2 * core)

    barrier = pltpu.get_barrier_semaphore()

    def greet(d, _):
        pl.semaphore_signal(barrier, inc=1, device_id=p_peer(d), device_id_type=MESH)
        return 0

    for d in (1, 7):
        pl.semaphore_signal(barrier, inc=1, device_id=y_peer(d), device_id_type=MESH)
        pl.semaphore_signal(barrier, inc=1, device_id=z_peer(d), device_id_type=MESH)
    lax.fori_loop(1, 8, greet, 0)

    def set_unit(rows):
        values = images[rows, :].astype(F32)
        norm = jnp.sqrt(jnp.sum(values * values, axis=1, keepdims=True) + EPS)
        unit[z, rows, :] = (values / norm).astype(BF16)

    def set_scale(vs):
        v = piece[vs].astype(F32)
        scale[vs] = (LOG2E / SHARP) / jnp.sqrt(jnp.sum(v * v, axis=0, keepdims=True) + EPS)

    proto_copy = pltpu.make_async_copy(proto, piece.at[y], in_sem.at[0])
    feat_copy = pltpu.make_async_copy(feat, images, in_sem.at[1])
    proto_copy.start()
    feat_copy.start()
    proto_copy.wait()
    pl.semaphore_wait(barrier, 11)

    def chunk(c):
        return pl.ds(c * (256 // CHUNKS), 256 // CHUNKS)

    def half_chunk(c):
        rows = 256 // CHUNKS
        return pl.ds(pl.multiple_of(core * HALF + c * rows, rows), rows)

    def way(r):
        return 1 if r == 0 else 7

    def piece_copy(r, s, c):
        slot = lax.rem(y + 8 * (s - 1) - way(r) * (s - 1), NY)
        return pltpu.make_async_remote_copy(
            src_ref=piece.at[slot, chunk(c)], dst_ref=piece.at[slot, chunk(c)],
            send_sem=piece_send, recv_sem=piece_recv.at[r, s, c],
            device_id=y_peer(way(r)), device_id_type=MESH)

    def unit_copy(r, s, c):
        slot = lax.rem(z + 8 * (s - 1) - way(r) * (s - 1), NZ)
        return pltpu.make_async_remote_copy(
            src_ref=unit.at[slot, half_chunk(c)], dst_ref=unit.at[slot, half_chunk(c)],
            send_sem=unit_send, recv_sem=unit_recv.at[r, s, c],
            device_id=z_peer(way(r)), device_id_type=MESH)

    def core_copy(r, s, c):
        slot = lax.rem(z + 8 * s - way(r) * s, NZ)
        return pltpu.make_async_remote_copy(
            src_ref=unit.at[slot, half_chunk(c)], dst_ref=unit.at[slot, half_chunk(c)],
            send_sem=core_send, recv_sem=core_recv.at[r, s, c],
            device_id=other_core, device_id_type=MESH)

    for c in range(CHUNKS):
        for r in range(2):
            piece_copy(r, 1, c).start()
    feat_copy.wait()
    set_unit(pl.ds(pl.multiple_of(core * HALF, HALF), HALF))
    for c in range(CHUNKS):
        for r in range(2):
            unit_copy(r, 1, c).start()
    set_unit(pl.ds(pl.multiple_of((1 - core) * HALF, HALF), HALF))
    set_scale(y)
    colacc[...] = jnp.zeros_like(colacc)
    wide[...] = jnp.zeros_like(wide)

    def slot_pair(t):
        k = sum((t >= j * j).astype(jnp.int32) for j in range(1, 8))
        rest = t - k * k
        ku = jnp.where(rest < k, rest, k)
        kv = jnp.where(rest < k, k, rest - k)
        return lax.rem(z - near_first(ku) + NZ, NZ), lax.rem(y - near_first(kv) + NY, NY)

    def blocks(b, _):
        for q in range(GROUP):
            us, vs = slot_pair(GROUP * b + q)
            e = jnp.exp2(jnp.dot(unit[us], piece[vs], preferred_element_type=F32) * scale[vs])
            tile[vs, pl.ds(pl.multiple_of(us * ROWS, ROWS), ROWS), :] = e
            colacc[vs] += jnp.sum(e.reshape(ROWS // 8, 8, COLS), axis=0)
        return 0

    def last_block(s):
        return s + (s >= 2).astype(jnp.int32) + 2 * (s >= 3).astype(jnp.int32)

    def arrive(s, _):
        for c in range(CHUNKS):
            for r in range(2):
                for copy in (piece_copy, unit_copy):
                    @pl.when(s + r <= 4)
                    def _():
                        copy(r, s, c).wait_recv()

                        @pl.when(s + r < 4)
                        def _():
                            copy(r, s + 1, c).start()

            for r in range(2):
                @pl.when(s + r <= 4)
                def _():
                    core_copy(r, s, c).start()

        @pl.when(s <= 4)
        def _():
            set_scale(lax.rem(y + 7 * s, NY))

        @pl.when(s < 4)
        def _():
            set_scale(lax.rem(y + s, NY))
            for c in range(CHUNKS):
                for r in range(2):
                    core_copy(r, s, c).wait_recv()

        @pl.when(s == 5)
        def _():
            for c in range(CHUNKS):
                core_copy(0, 4, c).wait_recv()

        lax.fori_loop(last_block(s - 1), last_block(s), blocks, 0)
        return 0

    lax.fori_loop(1, 6, arrive, 0)

    def col_copy(step, d):
        return pltpu.make_async_remote_copy(
            src_ref=colbuf.at[step, 0], dst_ref=colbuf.at[step, d],
            send_sem=col_send.at[step], recv_sem=col_recv.at[step],
            device_id=y_peer(d), device_id_type=MESH)

    def rowp_copy(step, h, d):
        part = pl.ds(h * PART, PART)
        return pltpu.make_async_remote_copy(
            src_ref=rowpart.at[part], dst_ref=rowbuf.at[step, h, d],
            send_sem=rowp_send.at[step], recv_sem=rowp_recv.at[step, h],
            device_id=p_peer(d), device_id_type=MESH)

    def rowz_copy(step, h, d):
        return pltpu.make_async_remote_copy(
            src_ref=rowall.at[step, h, 0], dst_ref=rowall.at[step, h, d],
            send_sem=rowz_send.at[step], recv_sem=rowz_recv.at[step, h],
            device_id=z_peer(d), device_id_type=MESH)

    def lastz_copy(d):
        return pltpu.make_async_remote_copy(
            src_ref=rowpart.at[lax.rem(z + d, NZ)], dst_ref=lastz.at[d],
            send_sem=rowz_send.at[ITERS - 1], recv_sem=rowz_recv.at[ITERS - 1, 0],
            device_id=z_peer(d), device_id_type=MESH)

    def lastp_copy(d):
        return pltpu.make_async_remote_copy(
            src_ref=lastp.at[me_p], dst_ref=lastp.at[me_p],
            send_sem=rowp_send.at[ITERS - 1], recv_sem=rowp_recv.at[ITERS - 1, 0],
            device_id=p_peer(d), device_id_type=MESH)

    def settle(ref, semaphore):
        pltpu.make_async_copy(ref, ref, semaphore).wait()

    def send_all(copy):
        for d in FAR_FIRST:
            copy(d).start()

    def rows_of(i, q):
        return pl.ds(pl.multiple_of(i * BLOCK + q * LANES, LANES), LANES)

    def column_pass(step):
        def spread(i):
            return [jnp.broadcast_to(weight[i, q:q + 1, :], (LANES, LANES)).T for q in range(PER)]

        def part_pass(h, acc):
            settle(rowall.at[step, h, 1:], rowz_recv.at[step, h])
            weight[pl.ds(h * PART, PART)] = 1.0 / (IMAGES * jnp.sum(rowall[step, h], axis=0))
            first = h * PART
            for q, w in enumerate(spread(first)):
                wide[0, q] = w

            def body(i, acc):
                acc = list(acc)
                ws = [wide[lax.rem(i, 2), q] for q in range(PER)]
                ahead = spread(first + jnp.minimum(i + 1, PART - 1)) if PART > 1 else []
                for q in range(PER):
                    for j in range(2 * NY):
                        t = tile[j // 2, rows_of(first + i, q), (j % 2) * LANES:(j % 2 + 1) * LANES] * ws[q]
                        acc[j] = acc[j] + jnp.sum(t.reshape(LANES // 8, 8, LANES), axis=0)
                for q, w in enumerate(ahead):
                    wide[1 - lax.rem(i, 2), q] = w
                return tuple(acc)

            return lax.fori_loop(0, PART, body, acc)

        acc = lax.fori_loop(0, SPLIT, part_pass, tuple(jnp.zeros((8, LANES), F32) for _ in range(2 * NY)))
        for j in range(2 * NY):
            colacc[j // 2, :, (j % 2) * LANES:(j % 2 + 1) * LANES] = acc[j]

    def row_pass(slot, done):
        def work(i):
            out = []
            for q in range(PER):
                acc = None
                for j in range(2 * NY):
                    lanes = slice((j % 2) * LANES, (j % 2 + 1) * LANES)
                    t = tile[j // 2, rows_of(slot(i), q), lanes] * colval[j // 2:j // 2 + 1, lanes]
                    acc = t if acc is None else acc + t
                out.append(acc)
            return out

        def finish(i):
            return [jnp.sum(wide[lax.rem(i, 2), q].T, axis=0, keepdims=True) for q in range(PER)]

        def put(i, sums):
            for q in range(PER):
                rowpart[slot(i), q:q + 1, :] = sums[q]

        def store(i, parts):
            for q in range(PER):
                wide[lax.rem(i, 2), q] = parts[q]

        def body(i, _):
            before = jnp.maximum(i - 1, 0)
            sums = finish(i + 1)
            parts = work(i)
            put(before, sums)
            store(i, parts)

            @pl.when((i > 0) & (lax.rem(i, PART) == 0))
            def _():
                done(i // PART - 1)

            return 0

        lax.fori_loop(0, NBLOCK, body, 0)
        put(NBLOCK - 1, finish(NBLOCK - 1))
        done(SPLIT - 1)

    def distance(i):
        return near_first(NBLOCK - 1 - i)

    def iteration(step, _):
        last = step == ITERS - 1

        @pl.when(step > 0)
        def _():
            column_pass(step - 1)

        colbuf[step, 0] = jnp.sum(colacc[...], axis=1)
        send_all(lambda d: col_copy(step, d))
        settle(colbuf.at[step, 1:], col_recv.at[step])
        colval[...] = 1.0 / (K * jnp.sum(colbuf[step], axis=0))

        def send_part(h):
            @pl.when(jnp.logical_not(last))
            def _():
                send_all(lambda d: rowp_copy(step, h, d))

            @pl.when(last)
            def _():
                for j in range(PART):
                    @pl.when(h * PART + j < NBLOCK - 1)
                    def _():
                        lastz_copy(distance(h * PART + j)).start()

        row_pass(lambda i: jnp.where(last, lax.rem(z + distance(i), NZ), i), send_part)

        @pl.when(jnp.logical_not(last))
        def _():
            def sum_part(h, _):
                settle(rowbuf.at[step, h, 1:], rowp_recv.at[step, h])
                rowall[step, h, 0] = rowpart[pl.ds(h * PART, PART)] + jnp.sum(rowbuf[step, h, 1:], axis=0)
                send_all(lambda d: rowz_copy(step, h, d))
                return 0

            lax.fori_loop(0, SPLIT, sum_part, 0)
            settle(rowbuf.at[step, :, 1:], rowp_send.at[step])

        return 0

    lax.fori_loop(0, ITERS, iteration, 0)
    settle(lastz.at[1:], rowz_recv.at[ITERS - 1, 0])
    lastp[pl.ds(me_p, 1)] = rowpart[pl.ds(z, 1)] + jnp.sum(lastz[1:], axis=0)[None]
    send_all(lastp_copy)
    settle(lastp.at[1:], rowp_recv.at[ITERS - 1, 0])
    row_out[...] = IMAGES * (1.0 / (IMAGES * jnp.sum(lastp[...], axis=0)))
    col_out[...] = float(K) * float(IMAGES) * colval[pl.ds(y, 1), :]

    settle(unit.at[1:, pl.ds(0, HALF)], unit_send)
    settle(unit.at[1:, pl.ds(0, HALF)], core_send)
    settle(piece.at[1:], piece_send)
    for step in range(ITERS):
        settle(colbuf.at[step, 1:], col_send.at[step])
    for step in range(ITERS - 1):
        settle(rowall.at[step, :, 1:], rowz_send.at[step])
    settle(lastz.at[1:], rowz_send.at[ITERS - 1])
    settle(lastp.at[1:], rowp_send.at[ITERS - 1])


def logs(row_mass, col_mass, row_log, col_log):
    row_log[...] = jnp.log(row_mass[...])
    col_log[...] = jnp.log(col_mass[...])


def local(features, prototypes):
    vmem = pl.BlockSpec(memory_space=pltpu.VMEM)
    row_mass, col_mass = pl.pallas_call(
        kernel,
        out_shape=(
            jax.ShapeDtypeStruct((ROWS // LANES, LANES), F32),
            jax.ShapeDtypeStruct((1, COLS), F32),
        ),
        in_specs=[pl.BlockSpec(memory_space=pltpu.HBM)] * 2,
        out_specs=(vmem, vmem),
        scratch_shapes=[
            pltpu.VMEM((ROWS, 256), BF16),
            pltpu.VMEM((NY, NZ * ROWS, COLS), F32),
            pltpu.VMEM((NZ, ROWS, 256), BF16),
            pltpu.VMEM((NY, 256, COLS), BF16),
            pltpu.VMEM((NY, 1, COLS), F32),
            pltpu.VMEM((NY, 8, COLS), F32),
            pltpu.VMEM((ITERS, NY, NY, COLS), F32),
            pltpu.VMEM((NY, COLS), F32),
            pltpu.VMEM((NZ, 4, LANES), F32),
            pltpu.VMEM((ITERS - 1, SPLIT, NP, PART, 4, LANES), F32),
            pltpu.VMEM((ITERS - 1, SPLIT, NZ, PART, 4, LANES), F32),
            pltpu.VMEM((NZ, 4, LANES), F32),
            pltpu.VMEM((NP, 4, LANES), F32),
            pltpu.VMEM((NZ, 4, LANES), F32),
            pltpu.VMEM((2, PER, LANES, LANES), F32),
        ]
        + [pltpu.SemaphoreType.DMA((2,))]
        + [pltpu.SemaphoreType.DMA, pltpu.SemaphoreType.DMA((2, 5, CHUNKS))] * 3
        + [pltpu.SemaphoreType.DMA((ITERS,))] * 2
        + [pltpu.SemaphoreType.DMA((ITERS,)), pltpu.SemaphoreType.DMA((ITERS, SPLIT))] * 2,
        compiler_params=pltpu.CompilerParams(
            collective_id=0, has_side_effects=True, vmem_limit_bytes=56 * 2**20
        ),
        cost_estimate=pl.CostEstimate(
            flops=2 * 4096 * 2048 * 256, bytes_accessed=2**20, transcendentals=4096 * 2048
        ),
        name="sinkhorn",
    )(features, prototypes)
    row_log, col_log = pl.pallas_call(
        logs,
        out_shape=(
            jax.ShapeDtypeStruct((ROWS // LANES, LANES), F32),
            jax.ShapeDtypeStruct((1, COLS), F32),
        ),
        in_specs=[vmem, vmem],
        out_specs=(vmem, vmem),
        name="logs",
    )(row_mass, col_mass)
    return row_log.reshape(ROWS), col_log.reshape(COLS)


def solution(mesh):
    in_specs = (P("dp", None), P(None, ("proto", "dp")))
    out_specs = (P("dp"), P(("proto", "dp")))
    return jax.shard_map(local, mesh=mesh, in_specs=in_specs, out_specs=out_specs, check_vma=False)
```
